32 devices in a mesh: req: 8 (over y, x, core), cache: 4 (over z).
Axes of the slice: x: 2, y: 2, z: 4, core: 2. Of those that a mesh axis runs over, the one named last changes fastest.
Arguments:
- cand_x: bfloat16 [8192, 1024], P(('req', 'cache')), may hold values from -6 to 6
- cand_req: int32 [8192, 1], P(('req', 'cache')), may hold values from 0 to 31; in each aligned block of 256 rows (0 to 255, 256 to 511, ...) at most 16 rows name the same one
- hist_len: int32 [32], P(('req', 'cache')), may hold values from 1 to 2048, 32768 in all
- block_place: int32 [32, 128], P(('req', 'cache')), may hold values from 0 to 127, each once within a row
- kv_store: bfloat16 [32, 32, 4, 16, 2048], P(('req', 'cache')), may hold values from -6 to 6
- store_bucket: int32 [32, 32, 4, 16], P(('req', 'cache')), may hold values from 1 to 127
- w_proj: bfloat16 [1024, 2048], replicated, may hold values from -0.1875 to 0.1875
- w_out: bfloat16 [1024, 1024], replicated, may hold values from -0.1875 to 0.1875
- time_bias: float32 [8, 128], replicated, may hold values from -4 to 4
Outputs:
- scored: bfloat16 [8192, 1024], P(('req', 'cache'))
The draws below stay inside these ranges and needn't reach their ends.
Inputs may be any that keep to these rules, and one draw needn't show every extreme that they name: `cand_req`: among the 256 candidate rows of one device at most 16 belong to one request, and some request of some device has exactly 16. `hist_len`: the lengths sum to 32768. `block_place`: each row is a permutation of 0 to 127.
All inputs are finite; a program needn't handle non-finite values. No bound on the sum of `hist_len` on one device may be relied on, other than what follows from the above.
Results may differ from the reference program's by a relative error of at most 0.0055.
Values may be sent and summed in bfloat16 or wider, within the bound.
A program may use at most 128 MiB of HBM per device.

```python
import math
import jax
import jax.numpy as jnp
import numpy as np
from jax import lax

D = 1024
HEADS = 8
HEAD_DIM = 128
NBUCKET = 128
BLOCK_EV = 16
MAXH = 2048
CAND_DEV = 256
NREQ = 32
NCAND = 8192
CAP = 16
SLOTS = 512
MAXB = 128
CAP_B = 4


def touch_ends(entries, rng, smallest, top_value):
    shape = entries.shape
    spot = [jax.random.randint(jax.random.fold_in(rng, axis), (), 0, shape[axis]) for axis in range(len(shape))]
    entries = entries.at[tuple(spot)].set(smallest)
    longest = shape.index(max(shape))
    spot[longest] = (spot[longest] + 1) % shape[longest]
    return entries.at[tuple(spot)].set(top_value)


def block_scale(stream_key, shape, pieces, low, high):
    factor_of, own = 1.0, jax.random.fold_in(stream_key, 6)
    for dim, blocks in pieces:
        heights = jnp.exp(jax.random.uniform(jax.random.fold_in(own, dim), (blocks,), jnp.float32, low / len(pieces), high / len(pieces)))
        factor_of = factor_of * jnp.repeat(heights, shape[dim] // blocks).reshape([-1 if axis == dim else 1 for axis in range(len(shape))])
    return factor_of


def profile(count, total, reach, skew):
    weights = [(1 << 20) // math.isqrt(standing ** skew) + 1 for standing in range(2, count + 1)]
    rest, counts = total - reach - (count - 1), [1] * (count - 1)
    while rest > 0:
        free = [i for i in range(count - 1) if counts[i] < reach]
        mass, left = sum([weights[i] for i in free]), rest
        for i in free:
            more = min(reach - counts[i], max(1, left * weights[i] // mass), rest)
            counts[i] = counts[i] + more
            rest = rest - more
    return np.array([reach] + counts)


def ragged(own_key, number_of, total, reach, lean):
    if number_of == 2:
        one = jax.random.randint(own_key, (), max(1, total - reach), min(reach, total - 1) + 1)
        return jnp.stack([one, total - one])
    lengths = jnp.asarray(profile(number_of, total, reach, lean), jnp.int32)
    pairs = (number_of - 1) // 2
    donor, taker = lengths[1:1 + 2 * pairs:2], lengths[2:2 + 2 * pairs:2]
    margin = jnp.minimum(donor - 1, reach - taker)
    moved = jax.random.randint(jax.random.fold_in(own_key, 1), (pairs,), 0, 1 << 20) % (margin + 1)
    lengths = lengths.at[1:1 + 2 * pairs:2].set(donor - moved).at[2:2 + 2 * pairs:2].set(taker + moved)
    return lengths[jax.random.permutation(jax.random.fold_in(own_key, 2), number_of)]


def routed_block(key, own, number, rows, count, top, most, lean):
    order = jax.random.permutation(key, count)
    packed, ordinary = portions_of(count, rows * top, most, lean, True), portions_of(count, rows * top, most, lean, False)
    places = jnp.arange(count)

    def named(lengths, turn):
        used = int((lengths > 0).sum())
        fixed = max(1, used // 4)
        moved = fixed + (places - fixed + turn * (used - fixed)) % max(1, count - fixed)
        return jnp.zeros((count,), jnp.int32).at[order[jnp.where(places < fixed, places, moved)]].set(jnp.asarray(lengths, jnp.int32))

    lengths = jnp.where(number % 4 == 0, named(packed, number // 4), named(ordinary, number - number // 4 - 1))
    mixed = jax.random.permutation(jax.random.fold_in(own, 3), count)
    giver, sink = mixed[0:count // 2 * 2:2], mixed[1:count // 2 * 2:2]
    room = jnp.minimum(lengths[giver] - 1, most - lengths[sink]) // 2
    room = jnp.where((giver == order[0]) | (sink == order[0]) | (lengths[sink] == 0), 0, jnp.maximum(room, 0))
    moved = jax.random.randint(jax.random.fold_in(own, 4), (count // 2,), 0, 1 << 20) % (room + 1)
    lengths = lengths.at[giver].add(-moved).at[sink].add(moved)
    labels = jnp.searchsorted(jnp.cumsum(lengths), jnp.arange(rows * top), side="right").astype(jnp.int32)
    table = labels.reshape(top, rows).T
    table = table[jax.random.permutation(jax.random.fold_in(own, 1), rows)]
    turn = jax.random.randint(jax.random.fold_in(own, 2), (rows, 1), 0, top)
    return jnp.take_along_axis(table, (jnp.arange(top)[None, :] + turn) % top, axis=1)


def portions_of(count, total, bound, skew, full):
    portions = [(1 << 20) // math.isqrt(standing ** skew) + 1 for standing in range(1, count + 1)]
    largest = bound if full else min(bound, max(-(-total // count), total * portions[0] // sum(portions)))
    least = 1 if total - largest >= count - 1 else 0
    holding, rest = [largest] + [least] * (count - 1), total - largest - least * (count - 1)
    while rest > 0:
        movable = [i for i in range(1, count) if holding[i] < largest] or [i for i in range(1, count) if holding[i] < bound]
        pool, left = sum([portions[i] for i in movable]), rest
        for i in movable:
            addition = min(bound - holding[i], max(1, left * portions[i] // pool), rest)
            holding[i] = holding[i] + addition
            rest = rest - addition
    return np.array(holding)


def gaussian(key, extent, scale, bound, cuts=(), kind=jnp.bfloat16):
    result = jax.random.normal(key, extent, jnp.float32) * scale
    if len(cuts) > 0:
        result = block_scale(key, extent, cuts, -0.22, 0.18) * result
    return jnp.clip(result, min=-bound, max=bound).astype(kind)


def setup_inputs(seed: int = 0) -> dict:
    key_list = jax.random.split(jax.random.key(seed), 10)
    cand_x = gaussian(key_list[0], (NCAND, D), 1.0, 6.0, ((0, 32),))
    cand_req_keys = jax.random.split(jax.random.fold_in(key_list[1], 1), NCAND // CAND_DEV)
    cand_req_turns = jax.random.permutation(jax.random.fold_in(key_list[1], 3), NCAND // CAND_DEV)
    cand_req = jax.vmap(lambda own, number: routed_block(jax.random.fold_in(key_list[1], 2), own, number, CAND_DEV, NREQ, 1, CAP, 1))(cand_req_keys, cand_req_turns).reshape((NCAND, 1))
    hist_len = ragged(key_list[2], NREQ, NREQ * MAXH // 2, MAXH, 2).astype(jnp.int32)
    block_place = jax.vmap(lambda own: jax.random.permutation(own, MAXB))(jax.random.split(key_list[3], NREQ)).reshape((NREQ, MAXB)).astype(jnp.int32)
    kv_store = gaussian(key_list[4], (NREQ, NREQ, CAP_B, BLOCK_EV, 2 * D), 1.0, 6.0, ((0, 32),))
    store_bucket = touch_ends(jax.random.randint(key_list[5], (NREQ, NREQ, CAP_B, BLOCK_EV), 1, NBUCKET), jax.random.fold_in(key_list[5], 1), 1, NBUCKET - 1).astype(jnp.int32)
    w_proj = gaussian(key_list[6], (D, 2 * D), D ** -0.5, 0.1875)
    w_out = gaussian(key_list[7], (D, D), D ** -0.5, 0.1875)
    time_bias = gaussian(key_list[8], (HEADS, NBUCKET), 1.0, 4.0, (), jnp.float32)
    return {"cand_x": cand_x, "cand_req": cand_req, "hist_len": hist_len, "block_place": block_place, "kv_store": kv_store, "store_bucket": store_bucket, "w_proj": w_proj, "w_out": w_out, "time_bias": time_bias}


def layer_norm(values):
    average = lax.optimization_barrier(jnp.mean(values, axis=-1, keepdims=True))
    centred = values - average
    spread = lax.optimization_barrier(jnp.mean(centred * centred, axis=-1, keepdims=True))
    return centred * lax.rsqrt(spread + 1e-05)

def reference(cand_x, cand_req, hist_len, block_place, kv_store, store_bucket, w_proj, w_out, time_bias):
    normed = layer_norm(cand_x.astype(jnp.float32)).astype(jnp.bfloat16)
    projected = jax.nn.silu(jnp.dot(normed, w_proj, preferred_element_type=jnp.float32)).astype(jnp.bfloat16)
    target = cand_req[:, 0].astype(jnp.int32)
    onehot = (target[:, None] == jnp.arange(NREQ, dtype=jnp.int32)[None, :]).astype(jnp.int32)
    onehot_blocks = onehot.reshape(NREQ, CAND_DEV, NREQ)
    earlier = jnp.cumsum(onehot_blocks, axis=1) - onehot_blocks
    slot_rank = lax.optimization_barrier(jnp.sum(earlier * onehot_blocks, axis=2)).reshape(NCAND).astype(jnp.int32)
    source = jnp.arange(NCAND, dtype=jnp.int32) // CAND_DEV
    flat_slot = (target * SLOTS + source * CAP + slot_rank).astype(jnp.int32)
    row_of_slot = jnp.full((NREQ * SLOTS,), NCAND, jnp.int32).at[flat_slot].set(jnp.arange(NCAND, dtype=jnp.int32))
    padded = jnp.concatenate([projected, jnp.zeros((1, 2 * D), jnp.bfloat16)], axis=0)
    score_scale = 1.0 / math.sqrt(HEAD_DIM)
    position = (jnp.arange(MAXB, dtype=jnp.int32)[:, None] * BLOCK_EV + jnp.arange(BLOCK_EV, dtype=jnp.int32)[None, :]).reshape(MAXH)

    def one_request(request):
        picked = lax.dynamic_slice_in_dim(row_of_slot, (request * SLOTS).astype(jnp.int32), SLOTS)
        slot_proj = jnp.take(padded, picked, axis=0)
        gate_u = slot_proj[:, :D].astype(jnp.float32)
        query = slot_proj[:, D:].astype(jnp.float32).reshape(SLOTS, HEADS, HEAD_DIM)
        places = block_place[request]
        owner = places // CAP_B
        inner = places % CAP_B
        blocks = kv_store[owner, request, inner]
        buckets = store_bucket[owner, request, inner].reshape(MAXH)
        live = (position < hist_len[request]).astype(jnp.float32)
        keys = blocks[:, :, :D].reshape(MAXH, HEADS, HEAD_DIM).astype(jnp.float32)
        values = blocks[:, :, D:].reshape(MAXH, HEADS, HEAD_DIM).astype(jnp.float32)
        bias = time_bias[:, buckets]
        scores = jnp.einsum('shd,ehd->hse', query, keys, precision=lax.Precision.HIGHEST) * score_scale + bias[:, None, :]
        weight = (jax.nn.silu(scores) * live[None, None, :]).astype(jnp.bfloat16)
        attended = jnp.einsum('hse,ehd->shd', weight.astype(jnp.float32), values, precision=lax.Precision.HIGHEST).reshape(SLOTS, D)
        hidden = (layer_norm(attended) * gate_u).astype(jnp.bfloat16)
        return jnp.dot(hidden, w_out, preferred_element_type=jnp.float32).astype(jnp.bfloat16)
    results = lax.map(one_request, jnp.arange(NREQ, dtype=jnp.int32))
    update = results.reshape(NREQ * SLOTS, D)[flat_slot]
    return (cand_x.astype(jnp.float32) + update.astype(jnp.float32)).astype(jnp.bfloat16)
```

```python
import functools
import math

import jax
import jax.numpy as jnp
from jax import lax
from jax.experimental import pallas as pl
from jax.experimental.pallas import tpu as pltpu
from jax.sharding import PartitionSpec as P


def layer_norm(values):
    average = jnp.mean(values, axis=-1, keepdims=True)
    centred = values - average
    spread = jnp.mean(centred * centred, axis=-1, keepdims=True)
    return centred * lax.rsqrt(spread + 1e-05)


def prepare(inputs, w_proj):
    normed = layer_norm(inputs.astype(jnp.float32)).astype(jnp.bfloat16)
    return jax.nn.silu(jnp.dot(normed, w_proj, preferred_element_type=jnp.float32)).astype(
        jnp.bfloat16
    )


def rank_of(target):
    index = jnp.arange(target.shape[0], dtype=jnp.int32)
    same = (target[:, None] == target[None, :]) & (index[None, :] < index[:, None])
    return jnp.sum(same.astype(jnp.int32), axis=1)


def send_back(update):
    return lax.all_to_all(update, ("req", "cache"), split_axis=0, concat_axis=0, tiled=True)


def shards(
    cand_x, cand_req, hist_len, block_place, kv_store, store_bucket, w_proj, w_out, time_bias
):
    devices = lax.axis_size(("req", "cache"))
    row_count = cand_x.shape[0]
    features = cand_x.shape[1]
    head_count = time_bias.shape[0]
    head_dim = features // head_count
    bucket_count = time_bias.shape[1]
    per_owner = kv_store.shape[2]
    block_ev = kv_store.shape[3]
    capacity = max(2, 2 * row_count // devices)
    arrived, arrived_bucket = (
        lax.all_to_all(kv_store, ("req", "cache"), split_axis=1, concat_axis=0, tiled=True),
        lax.all_to_all(store_bucket, ("req", "cache"), split_axis=1, concat_axis=0, tiled=True),
    )
    event_count = devices * per_owner * block_ev
    events = arrived.reshape(event_count, 2 * features)
    buckets = arrived_bucket.reshape(event_count)
    places = block_place[0]
    block_count = places.shape[0]
    block_ids = jnp.arange(block_count, dtype=jnp.int32)
    match = (places[:, None] == block_ids[None, :]).astype(jnp.int32)
    block_of_place = jnp.sum(match * block_ids[:, None], axis=0)
    position = (
        block_of_place[:, None] * block_ev + jnp.arange(block_ev, dtype=jnp.int32)[None, :]
    ).reshape(event_count)
    live = (position < hist_len[0]).astype(jnp.float32)
    bucket_table = (buckets[None, :] == jnp.arange(bucket_count, dtype=jnp.int32)[:, None]).astype(
        jnp.float32
    )
    bias = jnp.dot(time_bias, bucket_table, precision=lax.Precision.HIGHEST)
    score_scale = 1.0 / math.sqrt(head_dim)
    target = cand_req[:, 0]
    flat_slot = target * capacity + rank_of(target)
    empty = jnp.zeros((devices * capacity, cand_x.shape[1]), cand_x.dtype)
    received = lax.all_to_all(
        empty.at[flat_slot].set(cand_x).reshape(devices, capacity, cand_x.shape[1]),
        ("req", "cache"),
        split_axis=0,
        concat_axis=0,
        tiled=True,
    )
    senders = received.shape[0]
    item_count = received.shape[1]
    flat_rows = received.reshape(senders * item_count, features)
    projected = prepare(flat_rows, w_proj)
    slot_count = projected.shape[0]
    gate_u = projected[:, :features]
    query = projected[:, features:]

    def one_head(head_index):
        start = head_index * head_dim
        query_head = lax.dynamic_slice_in_dim(query, start, head_dim, 1)
        key_head = lax.dynamic_slice_in_dim(events, start, head_dim, 1)
        value_head = lax.dynamic_slice_in_dim(events, features + start, head_dim, 1)
        bias_head = lax.dynamic_slice_in_dim(bias, head_index, 1, 0)
        scores = lax.dot_general(
            query_head, key_head, (((1,), (1,)), ((), ())), preferred_element_type=jnp.float32
        )
        weight = (jax.nn.silu(scores * score_scale + bias_head) * live[None, :]).astype(
            jnp.bfloat16
        )
        return jnp.dot(weight, value_head, preferred_element_type=jnp.float32)

    per_head = lax.map(one_head, jnp.arange(head_count, dtype=jnp.int32))
    attended = jnp.transpose(per_head, (1, 0, 2)).reshape(slot_count, features)
    hidden = (layer_norm(attended) * gate_u.astype(jnp.float32)).astype(jnp.bfloat16)
    update = (
        jnp.dot(hidden, w_out, preferred_element_type=jnp.float32)
        .astype(jnp.bfloat16)
        .reshape(senders, item_count, features)
    )
    returned = send_back(update)
    update = returned.reshape(devices * capacity, features)[flat_slot]
    return (cand_x.astype(jnp.float32) + update.astype(jnp.float32)).astype(jnp.bfloat16)


MESH = pl.DeviceIdType.MESH
ANY = pl.BlockSpec(memory_space=pl.ANY)
VMEM = pl.BlockSpec(memory_space=pltpu.VMEM)


def place():
    req, z = lax.axis_index("req"), lax.axis_index("cache")
    core = lax.rem(req, 2)
    x = lax.rem(req // 2, 2)
    y = req // 4
    return req, z, core, x, y


def greet(others):
    barrier = pltpu.get_barrier_semaphore()
    for other in others:
        pl.semaphore_signal(barrier, inc=1, device_id=other, device_id_type=MESH)
    pl.semaphore_wait(barrier, len(others))


def remote(src, dst, send, recv, device):
    return pltpu.make_async_remote_copy(
        src_ref=src,
        dst_ref=dst,
        send_sem=send,
        recv_sem=recv,
        device_id=device,
        device_id_type=MESH,
    )


def spread_kernel(
    q_ref, kv_ref, meta_ref, bucket_ref, qall, kvp, meta_all, bucket_p,
    local_sem, pair_send, pair_recv, meta_send, meta_recv,
    z_send, z_recv, a_send, a_recv, e_send, e_recv, f_send, f_recv,
):
    req, z, core, x, y = place()
    partner = (req + 1 - 2 * core, z)
    xn = (y * 4 + (1 - x) * 2 + core, z)
    yn = ((1 - y) * 4 + x * 2 + core, z)
    rows = q_ref.shape[0]
    half = q_ref.shape[1] // 2
    reqs, zs = lax.axis_size("req"), lax.axis_size("cache")
    others = []
    for step in range(1, reqs * zs):
        others.append((lax.rem(req + step // zs, reqs), lax.rem(z + step % zs, zs)))
    greet(others)

    def slot(zz, yy, xx):
        return (zz * 2 + yy) * 2 + xx

    mine = slot(z, y, x)
    my_cols = pl.ds(pl.multiple_of(core * half, half), half)
    other_start = pl.multiple_of((1 - core) * half, half)
    other_cols = pl.ds(other_start, half)
    other_values = pl.ds(pl.multiple_of(2 * half + (1 - core) * half, half), half)
    my_rows = pl.ds(pl.multiple_of(core * rows, rows), rows)
    pair = [
        remote(q_ref.at[:, other_cols], qall.at[mine, my_rows, :], pair_send.at[0], pair_recv.at[0], partner),
        remote(kv_ref.at[:, other_cols], kvp.at[0], pair_send.at[1], pair_recv.at[1], partner),
        remote(kv_ref.at[:, other_values], kvp.at[1], pair_send.at[2], pair_recv.at[2], partner),
        remote(bucket_ref, bucket_p, pair_send.at[3], pair_recv.at[3], partner),
    ]
    pair[0].start()
    own = pltpu.make_async_copy(q_ref.at[:, my_cols], qall.at[mine, my_rows, :], local_sem.at[0])
    own.start()
    own_meta = pltpu.make_async_copy(meta_ref, meta_all.at[req * zs + z], local_sem.at[1])
    own_meta.start()
    metas = []
    for step, other in enumerate(others):
        copy = remote(
            meta_ref, meta_all.at[req * zs + z], meta_send.at[step], meta_recv.at[step], other
        )
        metas.append(copy)
    own.wait()
    pair[0].wait_recv()

    first, second = pl.ds(0, rows), pl.ds(rows, rows)
    started = []

    def go(ref, send, recv, device):
        copy = remote(ref, ref, send, recv, device)
        copy.start()
        started.append(copy)
        return copy

    z_copies = [None]
    for j in range(1, zs):
        z_copies.append(go(qall.at[mine], z_send.at[j], z_recv.at[j], (req, lax.rem(z + j, zs))))
    hops = []
    forwards = []
    for j in range(zs + 1):
        if j < zs:
            zz = lax.rem(z - j + zs, zs)
            if j > 0:
                z_copies[j].wait_recv()
            here = slot(zz, y, x)
            hops.append((
                go(qall.at[here, first, :], a_send.at[0, j], a_recv.at[0, j], yn),
                go(qall.at[here, second, :], a_send.at[1, j], a_recv.at[1, j], xn),
            ))
            forwards.append(
                go(qall.at[here, first, :], e_send.at[0, j], e_recv.at[0, j], xn)
            )
            forwards.append(
                go(qall.at[here, second, :], e_send.at[1, j], e_recv.at[1, j], yn)
            )
        if j == 0:
            for copy in metas:
                copy.start()
            for copy in pair[1:]:
                copy.start()
        if j > 0:
            i = j - 1
            zz = lax.rem(z - i + zs, zs)
            hops[i][0].wait_recv()
            forwards.append(
                go(qall.at[slot(zz, 1 - y, x), first, :], f_send.at[0, i], f_recv.at[0, i], xn)
            )
            hops[i][1].wait_recv()
            forwards.append(
                go(qall.at[slot(zz, y, 1 - x), second, :], f_send.at[1, i], f_recv.at[1, i], yn)
            )
    for copy in forwards:
        copy.wait_recv()
    for copy in started:
        copy.wait_send()
    for copy in metas:
        copy.wait()
    own_meta.wait()
    pair[0].wait_send()
    for copy in pair[1:]:
        copy.wait()


def spread(query, kv, meta, buckets):
    rows, features = query.shape
    events = kv.shape[0]
    reqs, zs = lax.axis_size("req"), lax.axis_size("cache")
    devices = reqs * zs
    dma = pltpu.SemaphoreType.DMA
    return pl.pallas_call(
        spread_kernel,
        out_shape=(
            jax.ShapeDtypeStruct((devices // 2, 2 * rows, features // 2), query.dtype),
            jax.ShapeDtypeStruct((2, events, features // 2), kv.dtype),
            jax.ShapeDtypeStruct((devices,) + meta.shape, meta.dtype),
            jax.ShapeDtypeStruct(buckets.shape, buckets.dtype),
        ),
        in_specs=[ANY] * 4,
        out_specs=(ANY,) * 4,
        scratch_shapes=[
            dma((2,)), dma((4,)), dma((4,)), dma((devices - 1,)), dma((devices - 1,)),
            dma((zs,)), dma((zs,)), dma((2, zs)), dma((2, zs)), dma((2, zs)), dma((2, zs)),
            dma((2, zs)), dma((2, zs)),
        ],
        compiler_params=pltpu.CompilerParams(collective_id=0, has_side_effects=True),
    )(query, kv, meta, buckets)


def attend_kernel(scale, q_ref, slot_ref, k_ref, v_ref, bias_ref, live_ref, out_ref, slots):
    chips, chip_rows, cols = q_ref.shape
    requests, slot_rows, _ = slots.shape
    devices = slot_ref.shape[0]
    rows = chip_rows // 2
    cap = slot_rows // devices

    def chosen(d):
        ids = lax.broadcasted_iota(jnp.int32, (requests * cap, rows), 0)
        return jnp.where(ids == slot_ref[d], 1.0, 0.0).astype(jnp.bfloat16)

    @pl.loop(0, chips)
    def _(chip):
        for part in range(2):
            got = jnp.dot(
                chosen(chip * 2 + part),
                q_ref[chip, part * rows : (part + 1) * rows, :],
                preferred_element_type=jnp.float32,
            ).astype(jnp.bfloat16)
            start = pl.multiple_of((chip * 2 + part) * cap, cap)
            slots[:, pl.ds(start, cap), :] = got.reshape(requests, cap, cols)

    pair = 256
    count = k_ref.shape[1]
    zero = jnp.zeros((count, pair // 2), jnp.bfloat16)

    @pl.loop(0, requests)
    def _(q):
        for hp in range(cols // pair):
            span = slice(hp * pair, (hp + 1) * pair)

            def diagonal(block):
                return jnp.concatenate(
                    [
                        jnp.concatenate([block[:, : pair // 2], zero], axis=1),
                        jnp.concatenate([zero, block[:, pair // 2 :]], axis=1),
                    ],
                    axis=0,
                )

            scores = lax.dot_general(
                slots[q, :, span],
                diagonal(k_ref[q, :, span]),
                (((1,), (1,)), ((), ())),
                preferred_element_type=jnp.float32,
            )
            halved = scores * (0.5 * scale) + bias_ref[q, hp : hp + 1, :]
            weight = (halved + halved * jnp.tanh(halved)) * live_ref[q]
            slots[q, :, span] = jnp.dot(
                weight.astype(jnp.bfloat16),
                diagonal(v_ref[q, :, span]),
                preferred_element_type=jnp.float32,
            ).astype(jnp.bfloat16)

    @pl.loop(0, chips)
    def _(chip):
        for part in range(2):
            start = pl.multiple_of((chip * 2 + part) * cap, cap)
            block = slots[:, pl.ds(start, cap), :].reshape(requests * cap, cols)
            out_ref[chip, part * rows : (part + 1) * rows, :] = lax.dot_general(
                chosen(chip * 2 + part),
                block,
                (((0,), (0,)), ((), ())),
                preferred_element_type=jnp.float32,
            ).astype(jnp.bfloat16)


def attend(qall, slot_rows, keys, values, bias, live, scale, requests, cap):
    devices = slot_rows.shape[0]
    cols = qall.shape[2]
    return pl.pallas_call(
        functools.partial(attend_kernel, scale),
        out_shape=jax.ShapeDtypeStruct(qall.shape, jnp.bfloat16),
        in_specs=[VMEM] * 6,
        out_specs=VMEM,
        scratch_shapes=[pltpu.VMEM((requests, devices * cap, cols), jnp.bfloat16)],
        compiler_params=pltpu.CompilerParams(vmem_limit_bytes=58 * 2**20),
        cost_estimate=pl.CostEstimate(
            flops=2 * 10**10, bytes_accessed=24 * 2**20, transcendentals=8 * 10**6
        ),
    )(qall, slot_rows, keys, values, bias, live)


def collect_kernel(
    part, mine_out, theirs_out, got1, got2, sum1, sum2, got_z, total,
    s1, r1, s2, r2, sz, rz, sp, rp,
):
    req, z, core, x, y = place()
    partner = (req + 1 - 2 * core, z)
    xn = (y * 4 + (1 - x) * 2 + core, z)
    yn = ((1 - y) * 4 + x * 2 + core, z)
    zs = lax.axis_size("cache")
    rows = part.shape[1] // 2
    f32 = jnp.float32
    greet([partner, xn, yn] + [(req, lax.rem(z + j, zs)) for j in range(1, zs)])

    def slot(zz, yy, xx):
        return (zz * 2 + yy) * 2 + xx

    spans = (slice(0, rows), slice(rows, 2 * rows))
    windows = (pl.ds(0, rows), pl.ds(rows, rows))
    order = list(range(1, zs)) + [0]
    firsts, seconds, z_copies = {}, {}, {}
    for j in order:
        zz = lax.rem(z + j, zs)
        for k in range(2):
            for keep in (0, 1):
                for h in range(2):
                    if h == 0:
                        source = slot(zz, (y if keep else 1 - y), 1 - x)
                        target = xn
                    else:
                        source = slot(zz, 1 - y, (x if keep else 1 - x))
                        target = yn
                    if keep != k:
                        continue
                    copy = remote(
                        part.at[source, windows[h], :],
                        got1.at[j, h, keep],
                        s1.at[j, h, keep],
                        r1.at[j, h, keep],
                        target,
                    )
                    copy.start()
                    firsts[j, h, keep] = copy
    for step in range(len(order) + 1):
        if step < len(order):
            j = order[step]
            zz = lax.rem(z + j, zs)
            for h in range(2):
                firsts[j, h, 0].wait_recv()
                away = slot(zz, 1 - y, x) if h == 0 else slot(zz, y, 1 - x)
                sum1[j, h] = (
                    part[away, spans[h], :].astype(f32) + got1[j, h, 0].astype(f32)
                ).astype(jnp.bfloat16)
                copy = remote(
                    sum1.at[j, h], got2.at[j, h], s2.at[j, h], r2.at[j, h], yn if h == 0 else xn
                )
                copy.start()
                seconds[j, h] = copy
        if step > 0:
            j = order[step - 1]
            zz = lax.rem(z + j, zs)
            for h in range(2):
                firsts[j, h, 1].wait_recv()
                seconds[j, h].wait_recv()
                here = (
                    part[slot(zz, y, x), spans[h], :].astype(f32)
                    + got1[j, h, 1].astype(f32)
                    + got2[j, h].astype(f32)
                )
                if j == 0:
                    total[h] = here
                else:
                    sum2[j, h] = here.astype(jnp.bfloat16)
                    copy = remote(
                        sum2.at[j, h], got_z.at[j, h], sz.at[j, h], rz.at[j, h], (req, zz)
                    )
                    copy.start()
                    z_copies[j, h] = copy
    for h in range(2):
        for j in range(1, zs):
            z_copies[j, h].wait_recv()
            total[h] = total[h] + got_z[j, h].astype(f32)
    swap = remote(total.at[1 - core], theirs_out, sp.at[0], rp.at[0], partner)
    swap.start()
    mine_out[...] = total[core]
    for copies in (firsts, seconds, z_copies):
        for copy in copies.values():
            copy.wait_send()
    swap.wait()


def collect(part):
    rows, cols = part.shape[1] // 2, part.shape[2]
    zs = lax.axis_size("cache")
    dma = pltpu.SemaphoreType.DMA
    b16 = jnp.bfloat16
    return pl.pallas_call(
        collect_kernel,
        out_shape=(jax.ShapeDtypeStruct((rows, cols), jnp.float32),) * 2,
        in_specs=[VMEM],
        out_specs=(VMEM, VMEM),
        scratch_shapes=[
            pltpu.VMEM((zs, 2, 2, rows, cols), b16),
            pltpu.VMEM((zs, 2, rows, cols), b16),
            pltpu.VMEM((zs, 2, rows, cols), b16),
            pltpu.VMEM((zs, 2, rows, cols), b16),
            pltpu.VMEM((zs, 2, rows, cols), b16),
            pltpu.VMEM((2, rows, cols), jnp.float32),
            dma((zs, 2, 2)), dma((zs, 2, 2)), dma((zs, 2)), dma((zs, 2)),
            dma((zs, 2)), dma((zs, 2)), dma((1,)), dma((1,)),
        ],
        compiler_params=pltpu.CompilerParams(
            collective_id=1, has_side_effects=True, vmem_limit_bytes=48 * 2**20
        ),
    )(part)


def gathered(
    cand_x, cand_req, hist_len, block_place, kv_store, store_bucket, w_proj, w_out, time_bias
):
    reqs, zs = lax.axis_size("req"), lax.axis_size("cache")
    devices = reqs * zs
    rows, features = cand_x.shape
    heads, bucket_count = time_bias.shape
    half_heads = heads // 2
    per_owner, block_ev = kv_store.shape[2], kv_store.shape[3]
    own_events = per_owner * block_ev
    requests = kv_store.shape[1]
    cap = max(2, 2 * rows // devices)
    req, z, core, _, _ = place()

    places = block_place[0]
    blocks = places.shape[0]
    ids = jnp.arange(blocks, dtype=jnp.int32)
    match = (places[:, None] == ids[None, :]).astype(jnp.int32)
    block_of_place = jnp.sum(match * ids[:, None], axis=0)
    alive = jnp.clip(hist_len[0] - block_of_place * block_ev, 0, block_ev)
    target = cand_req[:, 0]
    flat_slot = target * cap + rank_of(target)
    meta = jnp.concatenate(
        [alive, flat_slot, jnp.zeros((8 * 128 - blocks - rows,), jnp.int32)]
    ).reshape(8, 128)

    projected = prepare(cand_x, w_proj)
    gate_u = projected[:, :features]
    query = projected[:, features:]
    kv = kv_store.reshape(requests * own_events, 2 * features)
    qall, kvp, meta_all, bucket_p = spread(
        query, kv, meta, store_bucket.reshape(requests * own_events // 128, 128)
    )

    half = features // 2
    info = meta_all.reshape(devices, 8 * 128)
    slot_rows = info[:, blocks : blocks + rows].reshape(2, 2, 2, zs, rows)
    slot_rows = jnp.transpose(slot_rows, (3, 0, 1, 2, 4)).reshape(devices, 1, rows)
    alive_all = info[:, :blocks].reshape(devices, devices // 2 * 2, per_owner)
    me = req * zs + z
    other = (req + 1 - 2 * core) * zs + z
    event = jnp.arange(block_ev, dtype=jnp.int32)

    def live_of(owner):
        counts = lax.dynamic_slice_in_dim(alive_all, owner, 1, 1)[:, 0, :]
        return (event[None, None, :] < counts[:, :, None]).reshape(devices, own_events)

    live = jnp.concatenate([live_of(me), live_of(other)], axis=1).astype(jnp.float32)
    buckets = jnp.concatenate(
        [store_bucket.reshape(requests, own_events), bucket_p.reshape(requests, own_events)], axis=1
    )
    events = 2 * own_events
    table = (
        buckets.reshape(1, requests * events)
        == jnp.arange(bucket_count, dtype=jnp.int32)[:, None]
    ).astype(jnp.float32)
    my_bias = lax.dynamic_slice_in_dim(time_bias, core * half_heads, half_heads, 0)
    bias = 0.5 * jnp.dot(my_bias, table, precision=lax.Precision.HIGHEST)
    bias = jnp.transpose(bias.reshape(half_heads, requests, events), (1, 0, 2))
    bias = bias.reshape(requests, half_heads // 2, 2 * events)
    live = jnp.concatenate([live, live], axis=1).reshape(requests, 1, 2 * events)

    def joined(start, received):
        mine = lax.dynamic_slice_in_dim(kv, start + core * half, half, 1)
        return jnp.concatenate(
            [
                mine.reshape(requests, own_events, half),
                received.reshape(requests, own_events, half),
            ],
            axis=1,
        )

    part = attend(
        qall, slot_rows, joined(0, kvp[0]), joined(features, kvp[1]), bias, live,
        1.0 / math.sqrt(features // heads), requests, cap,
    )
    mine, theirs = collect(part)
    attended = jnp.where(
        core == 0,
        jnp.concatenate([mine, theirs], axis=1),
        jnp.concatenate([theirs, mine], axis=1),
    )
    hidden = (layer_norm(attended) * gate_u.astype(jnp.float32)).astype(jnp.bfloat16)
    update = jnp.dot(hidden, w_out, preferred_element_type=jnp.float32).astype(jnp.bfloat16)
    return (cand_x.astype(jnp.float32) + update.astype(jnp.float32)).astype(jnp.bfloat16)


def solution(mesh):
    placed = (
        P(("req", "cache"), None),
        P(("req", "cache"), None),
        P(("req", "cache")),
        P(("req", "cache"), None),
        P(("req", "cache"), None, None, None, None),
        P(("req", "cache"), None, None, None),
        P(),
        P(),
        P(),
    )
    body = gathered if mesh.shape["req"] == 8 and mesh.shape["cache"] == 4 else shards
    return jax.shard_map(
        body, mesh=mesh, in_specs=placed, out_specs=P(("req", "cache"), None), check_vma=False
    )
```

```python
import functools
import math

import jax
import jax.numpy as jnp
from jax import lax
from jax.experimental import pallas as pl
from jax.experimental.pallas import tpu as pltpu
from jax.sharding import PartitionSpec as P


def layer_norm(values):
    average = jnp.mean(values, axis=-1, keepdims=True)
    centred = values - average
    spread = jnp.mean(centred * centred, axis=-1, keepdims=True)
    return centred * lax.rsqrt(spread + 1e-05)


def prepare(inputs, w_proj):
    normed = layer_norm(inputs.astype(jnp.float32)).astype(jnp.bfloat16)
    return jax.nn.silu(jnp.dot(normed, w_proj, preferred_element_type=jnp.float32)).astype(
        jnp.bfloat16
    )


def rank_of(target):
    index = jnp.arange(target.shape[0], dtype=jnp.int32)
    same = (target[:, None] == target[None, :]) & (index[None, :] < index[:, None])
    return jnp.sum(same.astype(jnp.int32), axis=1)


def send_back(update):
    return lax.all_to_all(update, ("req", "cache"), split_axis=0, concat_axis=0, tiled=True)


def shards(
    cand_x, cand_req, hist_len, block_place, kv_store, store_bucket, w_proj, w_out, time_bias
):
    devices = lax.axis_size(("req", "cache"))
    row_count = cand_x.shape[0]
    features = cand_x.shape[1]
    head_count = time_bias.shape[0]
    head_dim = features // head_count
    bucket_count = time_bias.shape[1]
    per_owner = kv_store.shape[2]
    block_ev = kv_store.shape[3]
    capacity = max(2, 2 * row_count // devices)
    arrived, arrived_bucket = (
        lax.all_to_all(kv_store, ("req", "cache"), split_axis=1, concat_axis=0, tiled=True),
        lax.all_to_all(store_bucket, ("req", "cache"), split_axis=1, concat_axis=0, tiled=True),
    )
    event_count = devices * per_owner * block_ev
    events = arrived.reshape(event_count, 2 * features)
    buckets = arrived_bucket.reshape(event_count)
    places = block_place[0]
    block_count = places.shape[0]
    block_ids = jnp.arange(block_count, dtype=jnp.int32)
    match = (places[:, None] == block_ids[None, :]).astype(jnp.int32)
    block_of_place = jnp.sum(match * block_ids[:, None], axis=0)
    position = (
        block_of_place[:, None] * block_ev + jnp.arange(block_ev, dtype=jnp.int32)[None, :]
    ).reshape(event_count)
    live = (position < hist_len[0]).astype(jnp.float32)
    bucket_table = (buckets[None, :] == jnp.arange(bucket_count, dtype=jnp.int32)[:, None]).astype(
        jnp.float32
    )
    bias = jnp.dot(time_bias, bucket_table, precision=lax.Precision.HIGHEST)
    score_scale = 1.0 / math.sqrt(head_dim)
    target = cand_req[:, 0]
    flat_slot = target * capacity + rank_of(target)
    empty = jnp.zeros((devices * capacity, cand_x.shape[1]), cand_x.dtype)
    received = lax.all_to_all(
        empty.at[flat_slot].set(cand_x).reshape(devices, capacity, cand_x.shape[1]),
        ("req", "cache"),
        split_axis=0,
        concat_axis=0,
        tiled=True,
    )
    senders = received.shape[0]
    item_count = received.shape[1]
    flat_rows = received.reshape(senders * item_count, features)
    projected = prepare(flat_rows, w_proj)
    slot_count = projected.shape[0]
    gate_u = projected[:, :features]
    query = projected[:, features:]

    def one_head(head_index):
        start = head_index * head_dim
        query_head = lax.dynamic_slice_in_dim(query, start, head_dim, 1)
        key_head = lax.dynamic_slice_in_dim(events, start, head_dim, 1)
        value_head = lax.dynamic_slice_in_dim(events, features + start, head_dim, 1)
        bias_head = lax.dynamic_slice_in_dim(bias, head_index, 1, 0)
        scores = lax.dot_general(
            query_head, key_head, (((1,), (1,)), ((), ())), preferred_element_type=jnp.float32
        )
        weight = (jax.nn.silu(scores * score_scale + bias_head) * live[None, :]).astype(
            jnp.bfloat16
        )
        return jnp.dot(weight, value_head, preferred_element_type=jnp.float32)

    per_head = lax.map(one_head, jnp.arange(head_count, dtype=jnp.int32))
    attended = jnp.transpose(per_head, (1, 0, 2)).reshape(slot_count, features)
    hidden = (layer_norm(attended) * gate_u.astype(jnp.float32)).astype(jnp.bfloat16)
    update = (
        jnp.dot(hidden, w_out, preferred_element_type=jnp.float32)
        .astype(jnp.bfloat16)
        .reshape(senders, item_count, features)
    )
    returned = send_back(update)
    update = returned.reshape(devices * capacity, features)[flat_slot]
    return (cand_x.astype(jnp.float32) + update.astype(jnp.float32)).astype(jnp.bfloat16)


MESH = pl.DeviceIdType.MESH
ANY = pl.BlockSpec(memory_space=pl.ANY)
VMEM = pl.BlockSpec(memory_space=pltpu.VMEM)


def place():
    req, z = lax.axis_index("req"), lax.axis_index("cache")
    core = lax.rem(req, 2)
    x = lax.rem(req // 2, 2)
    y = req // 4
    return req, z, core, x, y


def greet(others):
    barrier = pltpu.get_barrier_semaphore()
    for other in others:
        pl.semaphore_signal(barrier, inc=1, device_id=other, device_id_type=MESH)
    pl.semaphore_wait(barrier, len(others))


def remote(src, dst, send, recv, device):
    return pltpu.make_async_remote_copy(
        src_ref=src,
        dst_ref=dst,
        send_sem=send,
        recv_sem=recv,
        device_id=device,
        device_id_type=MESH,
    )


def spread_kernel(
    q_ref, kv_ref, meta_ref, bucket_ref, qall, kvp, meta_all, bucket_p,
    local_sem, pair_send, pair_recv, meta_send, meta_recv,
    z_send, z_recv, a_send, a_recv, e_send, e_recv, f_send, f_recv,
):
    req, z, core, x, y = place()
    partner = (req + 1 - 2 * core, z)
    xn = (y * 4 + (1 - x) * 2 + core, z)
    yn = ((1 - y) * 4 + x * 2 + core, z)
    rows = q_ref.shape[0]
    half = q_ref.shape[1] // 2
    reqs, zs = lax.axis_size("req"), lax.axis_size("cache")
    others = []
    for step in range(1, reqs * zs):
        others.append((lax.rem(req + step // zs, reqs), lax.rem(z + step % zs, zs)))
    greet(others)

    def slot(zz, yy, xx):
        return (zz * 2 + yy) * 2 + xx

    mine = slot(z, y, x)
    my_cols = pl.ds(pl.multiple_of(core * half, half), half)
    other_start = pl.multiple_of((1 - core) * half, half)
    other_cols = pl.ds(other_start, half)
    other_values = pl.ds(pl.multiple_of(2 * half + (1 - core) * half, half), half)
    my_rows = pl.ds(pl.multiple_of(core * rows, rows), rows)
    pair = [
        remote(q_ref.at[:, other_cols], qall.at[mine, my_rows, :], pair_send.at[0], pair_recv.at[0], partner),
        remote(kv_ref.at[:, other_cols], kvp.at[0], pair_send.at[1], pair_recv.at[1], partner),
        remote(kv_ref.at[:, other_values], kvp.at[1], pair_send.at[2], pair_recv.at[2], partner),
        remote(bucket_ref, bucket_p, pair_send.at[3], pair_recv.at[3], partner),
    ]
    pair[0].start()
    own = pltpu.make_async_copy(q_ref.at[:, my_cols], qall.at[mine, my_rows, :], local_sem.at[0])
    own.start()
    own_meta = pltpu.make_async_copy(meta_ref, meta_all.at[req * zs + z], local_sem.at[1])
    own_meta.start()
    metas = []
    for step, other in enumerate(others):
        copy = remote(
            meta_ref, meta_all.at[req * zs + z], meta_send.at[step], meta_recv.at[step], other
        )
        metas.append(copy)
    own.wait()
    pair[0].wait_recv()

    first, second = pl.ds(0, rows), pl.ds(rows, rows)
    started = []

    def go(ref, send, recv, device):
        copy = remote(ref, ref, send, recv, device)
        copy.start()
        started.append(copy)
        return copy

    spans = (first, second)
    z_copies = {}
    for h in range(2):
        for j in range(1, zs):
            z_copies[h, j] = go(
                qall.at[mine, spans[h], :], z_send.at[h, j], z_recv.at[h, j],
                (req, lax.rem(z + j, zs)),
            )
    hops = []
    forwards = []
    order = [(0, 0), (1, 0)] + [(h, j) for h in range(2) for j in range(1, zs)]
    for step in range(len(order) + 1):
        if step < len(order):
            h, j = order[step]
            if j > 0:
                z_copies[h, j].wait_recv()
            here = slot(lax.rem(z - j + zs, zs), y, x)
            near, far = (yn, xn) if h == 0 else (xn, yn)
            hops.append(go(qall.at[here, spans[h], :], a_send.at[h, j], a_recv.at[h, j], near))
            forwards.append(
                go(qall.at[here, spans[h], :], e_send.at[h, j], e_recv.at[h, j], far)
            )
        if step == 1:
            for copy in metas:
                copy.start()
            for copy in pair[1:]:
                copy.start()
        if step > 0:
            h, j = order[step - 1]
            zz = lax.rem(z - j + zs, zs)
            away = slot(zz, 1 - y, x) if h == 0 else slot(zz, y, 1 - x)
            hops[step - 1].wait_recv()
            forwards.append(
                go(qall.at[away, spans[h], :], f_send.at[h, j], f_recv.at[h, j], xn if h == 0 else yn)
            )
    for copy in forwards:
        copy.wait_recv()
    for copy in started:
        copy.wait_send()
    for copy in metas:
        copy.wait()
    own_meta.wait()
    pair[0].wait_send()
    for copy in pair[1:]:
        copy.wait()


def spread(query, kv, meta, buckets):
    rows, features = query.shape
    events = kv.shape[0]
    reqs, zs = lax.axis_size("req"), lax.axis_size("cache")
    devices = reqs * zs
    dma = pltpu.SemaphoreType.DMA
    return pl.pallas_call(
        spread_kernel,
        out_shape=(
            jax.ShapeDtypeStruct((devices // 2, 2 * rows, features // 2), query.dtype),
            jax.ShapeDtypeStruct((2, events, features // 2), kv.dtype),
            jax.ShapeDtypeStruct((devices,) + meta.shape, meta.dtype),
            jax.ShapeDtypeStruct(buckets.shape, buckets.dtype),
        ),
        in_specs=[ANY] * 4,
        out_specs=(ANY,) * 4,
        scratch_shapes=[
            dma((2,)), dma((4,)), dma((4,)), dma((devices - 1,)), dma((devices - 1,)),
            dma((2, zs)), dma((2, zs)), dma((2, zs)), dma((2, zs)), dma((2, zs)), dma((2, zs)),
            dma((2, zs)), dma((2, zs)),
        ],
        compiler_params=pltpu.CompilerParams(collective_id=0, has_side_effects=True),
    )(query, kv, meta, buckets)


def attend_kernel(scale, q_ref, slot_ref, k_ref, v_ref, bias_ref, live_ref, out_ref, slots):
    chips, chip_rows, cols = q_ref.shape
    requests, slot_rows, _ = slots.shape
    devices = slot_ref.shape[0]
    rows = chip_rows // 2
    cap = slot_rows // devices

    def chosen(d):
        ids = lax.broadcasted_iota(jnp.int32, (requests * cap, rows), 0)
        return jnp.where(ids == slot_ref[d], 1.0, 0.0).astype(jnp.bfloat16)

    @pl.loop(0, chips)
    def _(chip):
        for part in range(2):
            got = jnp.dot(
                chosen(chip * 2 + part),
                q_ref[chip, part * rows : (part + 1) * rows, :],
                preferred_element_type=jnp.float32,
            ).astype(jnp.bfloat16)
            start = pl.multiple_of((chip * 2 + part) * cap, cap)
            slots[:, pl.ds(start, cap), :] = got.reshape(requests, cap, cols)

    pair = 256
    count = k_ref.shape[1]
    zero = jnp.zeros((count, pair // 2), jnp.bfloat16)

    @pl.loop(0, requests)
    def _(q):
        for hp in range(cols // pair):
            span = slice(hp * pair, (hp + 1) * pair)

            def diagonal(block):
                return jnp.concatenate(
                    [
                        jnp.concatenate([block[:, : pair // 2], zero], axis=1),
                        jnp.concatenate([zero, block[:, pair // 2 :]], axis=1),
                    ],
                    axis=0,
                )

            scores = lax.dot_general(
                slots[q, :, span],
                diagonal(k_ref[q, :, span]),
                (((1,), (1,)), ((), ())),
                preferred_element_type=jnp.float32,
            )
            halved = scores * (0.5 * scale) + bias_ref[q, hp : hp + 1, :]
            weight = (halved + halved * jnp.tanh(halved)) * live_ref[q]
            slots[q, :, span] = jnp.dot(
                weight.astype(jnp.bfloat16),
                diagonal(v_ref[q, :, span]),
                preferred_element_type=jnp.float32,
            ).astype(jnp.bfloat16)

    @pl.loop(0, chips)
    def _(chip):
        for part in range(2):
            start = pl.multiple_of((chip * 2 + part) * cap, cap)
            block = slots[:, pl.ds(start, cap), :].reshape(requests * cap, cols)
            out_ref[chip, part * rows : (part + 1) * rows, :] = lax.dot_general(
                chosen(chip * 2 + part),
                block,
                (((0,), (0,)), ((), ())),
                preferred_element_type=jnp.float32,
            ).astype(jnp.bfloat16)


def attend(qall, slot_rows, keys, values, bias, live, scale, requests, cap):
    devices = slot_rows.shape[0]
    cols = qall.shape[2]
    return pl.pallas_call(
        functools.partial(attend_kernel, scale),
        out_shape=jax.ShapeDtypeStruct(qall.shape, jnp.bfloat16),
        in_specs=[VMEM] * 6,
        out_specs=VMEM,
        scratch_shapes=[pltpu.VMEM((requests, devices * cap, cols), jnp.bfloat16)],
        compiler_params=pltpu.CompilerParams(vmem_limit_bytes=58 * 2**20),
        cost_estimate=pl.CostEstimate(
            flops=2 * 10**10, bytes_accessed=24 * 2**20, transcendentals=8 * 10**6
        ),
    )(qall, slot_rows, keys, values, bias, live)


def collect_kernel(
    part, mine_out, theirs_out, got1, got2, sum1, sum2, got_z, total,
    s1, r1, s2, r2, sz, rz, sp, rp,
):
    req, z, core, x, y = place()
    partner = (req + 1 - 2 * core, z)
    xn = (y * 4 + (1 - x) * 2 + core, z)
    yn = ((1 - y) * 4 + x * 2 + core, z)
    zs = lax.axis_size("cache")
    rows = part.shape[1] // 2
    f32 = jnp.float32
    greet([partner, xn, yn] + [(req, lax.rem(z + j, zs)) for j in range(1, zs)])

    def slot(zz, yy, xx):
        return (zz * 2 + yy) * 2 + xx

    spans = (slice(0, rows), slice(rows, 2 * rows))
    windows = (pl.ds(0, rows), pl.ds(rows, rows))
    order = list(range(1, zs)) + [0]
    firsts, seconds, z_copies = {}, {}, {}

    def begin(j):
        zz = lax.rem(z + j, zs)
        for k in range(2):
            for keep in (0, 1):
                for h in range(2):
                    if h == 0:
                        source = slot(zz, (y if keep else 1 - y), 1 - x)
                        target = xn
                    else:
                        source = slot(zz, 1 - y, (x if keep else 1 - x))
                        target = yn
                    if keep != k:
                        continue
                    copy = remote(
                        part.at[source, windows[h], :],
                        got1.at[j, h, keep],
                        s1.at[j, h, keep],
                        r1.at[j, h, keep],
                        target,
                    )
                    copy.start()
                    firsts[j, h, keep] = copy

    begin(order[0])
    begin(order[1])
    for step in range(len(order) + 1):
        if step < len(order):
            j = order[step]
            zz = lax.rem(z + j, zs)
            for h in range(2):
                firsts[j, h, 0].wait_recv()
                away = slot(zz, 1 - y, x) if h == 0 else slot(zz, y, 1 - x)
                sum1[j, h] = (
                    part[away, spans[h], :].astype(f32) + got1[j, h, 0].astype(f32)
                ).astype(jnp.bfloat16)
                copy = remote(
                    sum1.at[j, h], got2.at[j, h], s2.at[j, h], r2.at[j, h], yn if h == 0 else xn
                )
                copy.start()
                seconds[j, h] = copy
            if step + 2 < len(order):
                begin(order[step + 2])
        if step > 0:
            j = order[step - 1]
            zz = lax.rem(z + j, zs)
            for h in range(2):
                firsts[j, h, 1].wait_recv()
                seconds[j, h].wait_recv()
                here = (
                    part[slot(zz, y, x), spans[h], :].astype(f32)
                    + got1[j, h, 1].astype(f32)
                    + got2[j, h].astype(f32)
                )
                if j == 0:
                    total[h] = here
                else:
                    sum2[j, h] = here.astype(jnp.bfloat16)
                    copy = remote(
                        sum2.at[j, h], got_z.at[j, h], sz.at[j, h], rz.at[j, h], (req, zz)
                    )
                    copy.start()
                    z_copies[j, h] = copy
    for h in range(2):
        for j in range(1, zs):
            z_copies[j, h].wait_recv()
            total[h] = total[h] + got_z[j, h].astype(f32)
    swap = remote(total.at[1 - core], theirs_out, sp.at[0], rp.at[0], partner)
    swap.start()
    mine_out[...] = total[core]
    for copies in (firsts, seconds, z_copies):
        for copy in copies.values():
            copy.wait_send()
    swap.wait()


def collect(part):
    rows, cols = part.shape[1] // 2, part.shape[2]
    zs = lax.axis_size("cache")
    dma = pltpu.SemaphoreType.DMA
    b16 = jnp.bfloat16
    return pl.pallas_call(
        collect_kernel,
        out_shape=(jax.ShapeDtypeStruct((rows, cols), jnp.float32),) * 2,
        in_specs=[VMEM],
        out_specs=(VMEM, VMEM),
        scratch_shapes=[
            pltpu.VMEM((zs, 2, 2, rows, cols), b16),
            pltpu.VMEM((zs, 2, rows, cols), b16),
            pltpu.VMEM((zs, 2, rows, cols), b16),
            pltpu.VMEM((zs, 2, rows, cols), b16),
            pltpu.VMEM((zs, 2, rows, cols), b16),
            pltpu.VMEM((2, rows, cols), jnp.float32),
            dma((zs, 2, 2)), dma((zs, 2, 2)), dma((zs, 2)), dma((zs, 2)),
            dma((zs, 2)), dma((zs, 2)), dma((1,)), dma((1,)),
        ],
        compiler_params=pltpu.CompilerParams(
            collective_id=1, has_side_effects=True, vmem_limit_bytes=48 * 2**20
        ),
    )(part)


def gathered(
    cand_x, cand_req, hist_len, block_place, kv_store, store_bucket, w_proj, w_out, time_bias
):
    reqs, zs = lax.axis_size("req"), lax.axis_size("cache")
    devices = reqs * zs
    rows, features = cand_x.shape
    heads, bucket_count = time_bias.shape
    half_heads = heads // 2
    per_owner, block_ev = kv_store.shape[2], kv_store.shape[3]
    own_events = per_owner * block_ev
    requests = kv_store.shape[1]
    cap = max(2, 2 * rows // devices)
    req, z, core, _, _ = place()

    places = block_place[0]
    blocks = places.shape[0]
    ids = jnp.arange(blocks, dtype=jnp.int32)
    match = (places[:, None] == ids[None, :]).astype(jnp.int32)
    block_of_place = jnp.sum(match * ids[:, None], axis=0)
    alive = jnp.clip(hist_len[0] - block_of_place * block_ev, 0, block_ev)
    target = cand_req[:, 0]
    flat_slot = target * cap + rank_of(target)
    meta = jnp.concatenate(
        [alive, flat_slot, jnp.zeros((8 * 128 - blocks - rows,), jnp.int32)]
    ).reshape(8, 128)

    projected = prepare(cand_x, w_proj)
    gate_u = projected[:, :features]
    query = projected[:, features:]
    kv = kv_store.reshape(requests * own_events, 2 * features)
    qall, kvp, meta_all, bucket_p = spread(
        query, kv, meta, store_bucket.reshape(requests * own_events // 128, 128)
    )

    half = features // 2
    info = meta_all.reshape(devices, 8 * 128)
    slot_rows = info[:, blocks : blocks + rows].reshape(2, 2, 2, zs, rows)
    slot_rows = jnp.transpose(slot_rows, (3, 0, 1, 2, 4)).reshape(devices, 1, rows)
    alive_all = info[:, :blocks].reshape(devices, devices // 2 * 2, per_owner)
    me = req * zs + z
    other = (req + 1 - 2 * core) * zs + z
    event = jnp.arange(block_ev, dtype=jnp.int32)

    def live_of(owner):
        counts = lax.dynamic_slice_in_dim(alive_all, owner, 1, 1)[:, 0, :]
        return (event[None, None, :] < counts[:, :, None]).reshape(devices, own_events)

    live = jnp.concatenate([live_of(me), live_of(other)], axis=1).astype(jnp.float32)
    buckets = jnp.concatenate(
        [store_bucket.reshape(requests, own_events), bucket_p.reshape(requests, own_events)], axis=1
    )
    events = 2 * own_events
    table = (
        buckets.reshape(1, requests * events)
        == jnp.arange(bucket_count, dtype=jnp.int32)[:, None]
    ).astype(jnp.float32)
    my_bias = lax.dynamic_slice_in_dim(time_bias, core * half_heads, half_heads, 0)
    bias = 0.5 * jnp.dot(my_bias, table, precision=lax.Precision.HIGHEST)
    bias = jnp.transpose(bias.reshape(half_heads, requests, events), (1, 0, 2))
    bias = bias.reshape(requests, half_heads // 2, 2 * events)
    live = jnp.concatenate([live, live], axis=1).reshape(requests, 1, 2 * events)

    def joined(start, received):
        mine = lax.dynamic_slice_in_dim(kv, start + core * half, half, 1)
        return jnp.concatenate(
            [
                mine.reshape(requests, own_events, half),
                received.reshape(requests, own_events, half),
            ],
            axis=1,
        )

    part = attend(
        qall, slot_rows, joined(0, kvp[0]), joined(features, kvp[1]), bias, live,
        1.0 / math.sqrt(features // heads), requests, cap,
    )
    mine, theirs = collect(part)
    attended = jnp.where(
        core == 0,
        jnp.concatenate([mine, theirs], axis=1),
        jnp.concatenate([theirs, mine], axis=1),
    )
    hidden = (layer_norm(attended) * gate_u.astype(jnp.float32)).astype(jnp.bfloat16)
    update = jnp.dot(hidden, w_out, preferred_element_type=jnp.float32).astype(jnp.bfloat16)
    return (cand_x.astype(jnp.float32) + update.astype(jnp.float32)).astype(jnp.bfloat16)


def solution(mesh):
    placed = (
        P(("req", "cache"), None),
        P(("req", "cache"), None),
        P(("req", "cache")),
        P(("req", "cache"), None),
        P(("req", "cache"), None, None, None, None),
        P(("req", "cache"), None, None, None),
        P(),
        P(),
        P(),
    )
    body = gathered if mesh.shape["req"] == 8 and mesh.shape["cache"] == 4 else shards
    return jax.shard_map(
        body, mesh=mesh, in_specs=placed, out_specs=P(("req", "cache"), None), check_vma=False
    )
```
